32 devices in a mesh: amp: 8 (over z, core), int: 4 (over y, x).
Axes of the slice: x: 2, y: 2, z: 4, core: 2. Of those that a mesh axis runs over, the one named last changes fastest.
Arguments:
- amps: bfloat16 [64, 4, 1000], P('amp', 'int'), may hold values from -6 to 6
- integrals: bfloat16 [8192, 4, 1000], P('amp', 'int'), may hold values from -0.25 to 0.25
- irrep_sizes: int32 [8], replicated, may hold values from 1 to 200, 1000 in all
- c_irreps: int32 [4], P('int'), may hold values from 0 to 7
Outputs:
- ladder: float32 [64, 8192], P('int', 'amp')
The draws below stay inside these ranges and needn't reach their ends.
Inputs may be any that keep to these rules, and one draw needn't show every extreme that they name: `irrep_sizes`: the sizes sum to 1000 and the largest is exactly 200.
All inputs are finite; a program needn't handle non-finite values.
Results may differ from the reference program's by a relative error of at most 0.0003.
Values may be sent and summed in bfloat16 or wider, within the bound.
A program may use at most 64 MiB of HBM per device.

```python
import math
import jax
import jax.numpy as jnp
import numpy as np
from jax import lax

NV = 1000
NIRR = 8
MOST = 200
AB_DEV = 1024
NC = 4
NIJ = 64
NAB = 8192


def set_ends(values, key, low, largest):
    place = [jax.random.randint(jax.random.fold_in(key, axis), (), 0, length) for axis, length in enumerate(values.shape)]
    longest = values.shape.index(max(values.shape))
    beside = place[:longest] + [(place[longest] + 1) % values.shape[longest]] + place[longest + 1:]
    return values.at[tuple(place)].set(low).at[tuple(beside)].set(largest)


def with_spikes(drawn, rng, source, target, blocks, factor):
    def block_of(position):
        return (jnp.arange(drawn.shape[position]) // (drawn.shape[position] // blocks)).reshape((-1,) + (1,) * (drawn.ndim - 1 - position))

    near = jax.random.permutation(rng, blocks)[block_of(target)]
    other_side = (block_of(target) + blocks // 2) % blocks
    return jnp.where((block_of(source) == near) | (block_of(source) == other_side), factor * drawn, drawn)


def block_levels(rng, dims, split, least, top_value):
    def one(dim, blocks):
        heights = jax.random.uniform(jax.random.fold_in(jax.random.fold_in(rng, 6), dim), (blocks,), jnp.float32, least / len(split), top_value / len(split))
        return jnp.repeat(jnp.exp(heights), dims[dim] // blocks).reshape((-1,) + (1,) * (len(dims) - dim - 1))

    factor_of = one(*split[0])
    for cut in split[1:]:
        factor_of = factor_of * one(*cut)
    return factor_of


def length_profile(amount, total, most, skew):
    weights = [(1 << 20) // math.isqrt(grade ** skew) + 1 for grade in range(2, amount + 1)]
    surplus, given = total - most - (amount - 1), [1] * (amount - 1)
    while surplus > 0:
        candidates = [i for i in range(amount - 1) if given[i] < most]
        pool, budget = sum([weights[i] for i in candidates]), surplus
        for i in candidates:
            addition = min(most - given[i], max(1, budget * weights[i] // pool), surplus)
            given[i] = given[i] + addition
            surplus = surplus - addition
    return np.array([most] + given)


def uneven_parts(own_key, count, total, bound, skew):
    if count == 2:
        one = jax.random.randint(own_key, (), max(1, total - bound), min(bound, total - 1) + 1)
        return jnp.stack([one, total - one])
    lengths = jnp.asarray(length_profile(count, total, bound, skew), jnp.int32)
    couples = (count - 1) // 2
    donor, taker = lengths[1:1 + 2 * couples:2], lengths[2:2 + 2 * couples:2]
    room = jnp.minimum(donor - 1, bound - taker)
    moved = jax.random.randint(jax.random.fold_in(own_key, 1), (couples,), 0, 1 << 20) % (room + 1)
    lengths = lengths.at[1:1 + 2 * couples:2].set(donor - moved).at[2:2 + 2 * couples:2].set(taker + moved)
    return lengths[jax.random.permutation(jax.random.fold_in(own_key, 2), count)]


def bell_draw(stream_key, dims, deviation, limit, shards=(), kind=jnp.bfloat16):
    gain = block_levels(stream_key, dims, shards, -0.22, 0.18) if shards else 1.0
    result = jax.random.normal(stream_key, dims, jnp.float32) * deviation * gain
    return jnp.minimum(jnp.maximum(result, -limit), limit).astype(kind)


def bell_draw_with(rng, extent, deviation, most, pieces, heavy, kind=jnp.bfloat16):
    drawn = deviation * jax.random.normal(rng, extent, jnp.float32)
    if pieces:
        drawn = drawn * block_levels(rng, extent, pieces, -0.22, 0.18)
    return jnp.clip(with_spikes(drawn, jax.random.fold_in(rng, 3), *heavy), -most, most).astype(kind)


def setup_inputs(seed: int = 0) -> dict:
    seeds = jax.random.split(jax.random.key(seed), 5)
    amps = bell_draw_with(seeds[0], (NIJ, NC, NV), 1.0, 6.0, ((0, 8), (1, 4)), (1, 0, 4, 2.0))
    integrals = bell_draw(seeds[1], (NAB, NC, NV), (NC * NV // NIRR) ** -0.5, 0.25, ((0, 8), (1, 4)))
    irrep_sizes = uneven_parts(seeds[2], NIRR, NV, MOST, 2).astype(jnp.int32)
    c_irreps = set_ends(jax.random.randint(seeds[3], (NC,), 0, NIRR), jax.random.fold_in(seeds[3], 1), 0, NIRR - 1).astype(jnp.int32)
    return {"amps": amps, "integrals": integrals, "irrep_sizes": irrep_sizes, "c_irreps": c_irreps}


def allowed_mask(irrep_sizes, c_irreps, width):
    ends = jnp.cumsum(irrep_sizes)
    column = jnp.arange(width, dtype=jnp.int32)
    d_irrep = jnp.sum((column[:, None] >= ends[None, :]).astype(jnp.int32), axis=1)
    return (d_irrep[None, :] == c_irreps[:, None]).astype(jnp.bfloat16)


def reference(amps, integrals, irrep_sizes, c_irreps):
    allowed = allowed_mask(irrep_sizes, c_irreps, NV)
    blocked = (amps * allowed[None, :, :]).astype(jnp.float32).reshape(NIJ, NC * NV)
    blocks = integrals.reshape(NAB // AB_DEV, AB_DEV, NC * NV)

    def one_block(block):
        return lax.dot_general(blocked, block.astype(jnp.float32), (((1,), (1,)), ((), ())), preferred_element_type=jnp.float32)

    parts = lax.map(one_block, blocks)
    return jnp.transpose(parts, (1, 0, 2)).reshape(NIJ, NAB)
```

```python
import functools

import jax
import jax.numpy as jnp
from jax import lax
from jax.experimental import pallas as pl
from jax.experimental.pallas import tpu as pltpu
from jax.sharding import PartitionSpec as P

MESH = pl.DeviceIdType.MESH
MOST = 200
TILE = 16
LANES = 128


def window_of(width):
    return width


def chunks_of(columns):
    return 4 if columns % (4 * LANES) == 0 else 1


def kernel(n_amp, n_int, sizes_hbm, irreps_hbm, amps_hbm, ints_hbm, out_ref, sizes, irreps, amps, ints, packed, gathered, part, landed,
           local_sem, g_send, g_recv, r_send, r_recv):
    me_a, me_i = lax.axis_index("amp"), lax.axis_index("int")
    c_local, rows, width = amps.shape
    columns = ints.shape[2]
    chunks, _, out_rows, chunk = part.shape
    win = window_of(width)
    pieces = packed.shape[0] // (c_local * rows)

    barrier = pltpu.get_barrier_semaphore()
    for k in range(1, n_amp):
        pl.semaphore_signal(barrier, inc=1, device_id={"amp": lax.rem(me_a + k, n_amp)}, device_id_type=MESH)
    for k in range(1, n_int):
        pl.semaphore_signal(barrier, inc=1, device_id={"int": lax.rem(me_i + k, n_int)}, device_id_type=MESH)
    small = [
        pltpu.make_async_copy(sizes_hbm, sizes, local_sem.at[2]),
        pltpu.make_async_copy(irreps_hbm, irreps, local_sem.at[3]),
        pltpu.make_async_copy(amps_hbm, amps, local_sem.at[0]),
    ]
    for copy in small:
        copy.start()
    ints_in = pltpu.make_async_copy(ints_hbm, ints, local_sem.at[1])
    ints_in.start()

    for copy in small:
        copy.wait()
    padded = -(-width // LANES) * LANES
    for c in range(c_local):
        irrep = irreps[c]
        start, end = jnp.int32(0), jnp.int32(0)
        for g in range(sizes.shape[0]):
            size = sizes[g]
            start += jnp.where(g < irrep, size, 0)
            end += jnp.where(g <= irrep, size, 0)
        wide = jnp.pad(amps[c].astype(jnp.float32), ((0, 0), (0, padded - width)))
        column = lax.broadcasted_iota(jnp.int32, (rows, padded), 1)
        wide = jnp.where((column >= start) & (column < end), wide, 0.0)
        stack = jnp.concatenate([wide[:, p * LANES:(p + 1) * LANES] for p in range(pieces)], axis=0)
        packed[c * pieces * rows:(c + 1) * pieces * rows, :] = stack.astype(jnp.bfloat16)

    pl.semaphore_wait(barrier, n_amp + n_int - 2)
    sends = []
    for k in range(1, n_amp):
        copy = pltpu.make_async_remote_copy(
            src_ref=packed, dst_ref=gathered.at[me_a], send_sem=g_send.at[k], recv_sem=g_recv.at[me_a],
            device_id={"amp": lax.rem(me_a + k, n_amp)}, device_id_type=MESH)
        copy.start()
        sends.append(copy)
    gathered[me_a] = packed[...]
    ints_in.wait()
    for k in range(1, n_amp):
        source = lax.rem(me_a + n_amp - k, n_amp)
        pltpu.make_async_remote_copy(
            src_ref=packed, dst_ref=gathered.at[source], send_sem=g_send.at[k], recv_sem=g_recv.at[source],
            device_id={"amp": source}, device_id_type=MESH).wait_recv()

    pages = gathered[...].astype(jnp.float32)
    lhs = []
    for c in range(c_local):
        at = [(c * pieces + p) * rows for p in range(pieces)]
        cut = [pages[:, r:r + rows, :].reshape(n_amp * rows, LANES).astype(jnp.bfloat16) for r in at]
        lhs.append(jnp.concatenate(cut, axis=1)[:, :win])
    for h in range(chunks):
        total = None
        for c in range(c_local):
            block = ints[c, :, h * chunk:(h + 1) * chunk]
            term = jnp.dot(lhs[c], block, preferred_element_type=jnp.float32)
            total = term if total is None else total + term
        part[h] = total.reshape(n_int, out_rows, chunk)
        for k in range(1, n_int):
            to = lax.rem(me_i + k, n_int)
            copy = pltpu.make_async_remote_copy(
                src_ref=part.at[h, to], dst_ref=landed.at[h, me_i], send_sem=r_send.at[h, k],
                recv_sem=r_recv.at[h, me_i], device_id={"int": to}, device_id_type=MESH)
            copy.start()
            sends.append(copy)
    for h in range(chunks):
        total = part[h, me_i]
        for k in range(1, n_int):
            source = lax.rem(me_i + n_int - k, n_int)
            pltpu.make_async_remote_copy(
                src_ref=part.at[h, source], dst_ref=landed.at[h, source], send_sem=r_send.at[h, k],
                recv_sem=r_recv.at[h, source], device_id={"int": source}, device_id_type=MESH).wait_recv()
            total = total + landed[h, source]
        out_ref[:, h * chunk:(h + 1) * chunk] = total
    for copy in sends:
        copy.wait_send()


def solution(mesh):
    n_amp, n_int = mesh.shape["amp"], mesh.shape["int"]

    def body(amps, integrals, irrep_sizes, c_irreps):
        rows, c_local, width = amps.shape
        columns = integrals.shape[0]
        out_rows = n_amp * rows // n_int
        chunks = chunks_of(columns)
        pieces = -(-window_of(width) // LANES)
        page = (c_local * pieces * rows, LANES)
        parts = (chunks, n_int, out_rows, columns // chunks)
        return pl.pallas_call(
            functools.partial(kernel, n_amp, n_int),
            out_shape=jax.ShapeDtypeStruct((out_rows, columns), jnp.float32),
            in_specs=[
                pl.BlockSpec(memory_space=pl.ANY),
            ] * 4,
            out_specs=pl.BlockSpec(memory_space=pltpu.VMEM),
            scratch_shapes=[
                pltpu.SMEM(irrep_sizes.shape, jnp.int32),
                pltpu.SMEM(c_irreps.shape, jnp.int32),
                pltpu.VMEM((c_local, rows, width), jnp.bfloat16),
                pltpu.VMEM((c_local, width, columns), jnp.bfloat16),
                pltpu.VMEM(page, jnp.bfloat16),
                pltpu.VMEM((n_amp,) + page, jnp.bfloat16),
                pltpu.VMEM(parts, jnp.float32),
                pltpu.VMEM(parts, jnp.float32),
                pltpu.SemaphoreType.DMA((4,)),
                pltpu.SemaphoreType.DMA((n_amp,)),
                pltpu.SemaphoreType.DMA((n_amp,)),
                pltpu.SemaphoreType.DMA((chunks, n_int)),
                pltpu.SemaphoreType.DMA((chunks, n_int)),
            ],
            compiler_params=pltpu.CompilerParams(
                collective_id=0, has_side_effects=True, vmem_limit_bytes=63 * 1024 * 1024
            ),
            cost_estimate=pl.CostEstimate(
                flops=2 * n_amp * rows * columns * width, bytes_accessed=2 * columns * width, transcendentals=0
            ),
        )(irrep_sizes, c_irreps, jnp.transpose(amps, (1, 0, 2)), jnp.transpose(integrals, (1, 2, 0)))

    placed = (P("amp", "int", None), P("amp", "int", None), P(), P("int"))
    return jax.shard_map(
        body, mesh=mesh, in_specs=placed, out_specs=P("int", "amp"), check_vma=False
    )
```

```python
import functools

import jax
import jax.numpy as jnp
from jax import lax
from jax.experimental import pallas as pl
from jax.experimental.pallas import tpu as pltpu
from jax.sharding import PartitionSpec as P

MESH = pl.DeviceIdType.MESH
MOST = 200
TILE = 16
LANES = 128


def tiles_of(width):
    tiles = -(-width // TILE)
    return tiles, min(tiles, -(-(MOST + TILE - 1) // TILE))


def levels_of(last):
    levels = []
    while sum(levels) < last:
        levels.insert(0, 2 * levels[0] if levels else 1)
    return levels


def shifted(parts, kept, levels, first):
    for i, step in enumerate(levels):
        need = kept + sum(levels[i + 1:])
        odd = lax.rem(lax.div(first, step), 2) == 1
        parts = [
            jnp.where(odd, parts[j + step], parts[j]) if j + step < len(parts) else parts[j]
            for j in range(min(need, len(parts)))
        ]
    return parts


def chunks_of(columns):
    return 4 if columns % (4 * LANES) == 0 else 1


def kernel(n_amp, n_int, sizes_hbm, irreps_hbm, amps_hbm, ints_hbm, out_ref, sizes, irreps, amps, ints, window, packed, gathered, part, landed,
           local_sem, g_send, g_recv, r_send, r_recv):
    me_a, me_i = lax.axis_index("amp"), lax.axis_index("int")
    c_local, rows, width = amps.shape
    columns = ints.shape[2]
    chunks, _, out_rows, chunk = part.shape
    tiles, kept = tiles_of(width)
    levels = levels_of(tiles - kept)
    win = kept * TILE
    pieces = packed.shape[0] // (c_local * rows)

    barrier = pltpu.get_barrier_semaphore()
    for k in range(1, n_amp):
        pl.semaphore_signal(barrier, inc=1, device_id={"amp": lax.rem(me_a + k, n_amp)}, device_id_type=MESH)
    for k in range(1, n_int):
        pl.semaphore_signal(barrier, inc=1, device_id={"int": lax.rem(me_i + k, n_int)}, device_id_type=MESH)
    small = [
        pltpu.make_async_copy(sizes_hbm, sizes, local_sem.at[2]),
        pltpu.make_async_copy(irreps_hbm, irreps, local_sem.at[3]),
        pltpu.make_async_copy(amps_hbm, amps, local_sem.at[0]),
    ]
    for copy in small:
        copy.start()
    ints_in = pltpu.make_async_copy(ints_hbm, ints, local_sem.at[1])
    ints_in.start()

    firsts = []
    for copy in small:
        copy.wait()
    padded = -(-width // LANES) * LANES
    for c in range(c_local):
        irrep = irreps[c]
        start, end = jnp.int32(0), jnp.int32(0)
        for g in range(sizes.shape[0]):
            size = sizes[g]
            start += jnp.where(g < irrep, size, 0)
            end += jnp.where(g <= irrep, size, 0)
        first = jnp.minimum(lax.div(start, TILE), tiles - kept)
        firsts.append(first)
        wide = jnp.pad(amps[c].astype(jnp.float32), ((0, 0), (0, padded - width)))
        column = lax.broadcasted_iota(jnp.int32, (rows, padded), 1)
        wide = jnp.where((column >= start) & (column < end), wide, 0.0)
        for step in levels:
            odd = lax.rem(lax.div(first, step), 2) == 1
            wide = jnp.where(odd, pltpu.roll(wide, padded - step * TILE, 1), wide)
        stack = jnp.concatenate([wide[:, p * LANES:(p + 1) * LANES] for p in range(pieces)], axis=0)
        packed[c * pieces * rows:(c + 1) * pieces * rows, :] = stack.astype(jnp.bfloat16)

    pl.semaphore_wait(barrier, n_amp + n_int - 2)
    sends = []
    for k in range(1, n_amp):
        copy = pltpu.make_async_remote_copy(
            src_ref=packed, dst_ref=gathered.at[me_a], send_sem=g_send.at[k], recv_sem=g_recv.at[me_a],
            device_id={"amp": lax.rem(me_a + k, n_amp)}, device_id_type=MESH)
        copy.start()
        sends.append(copy)
    gathered[me_a] = packed[...]
    ints_in.wait()
    for c in range(c_local):
        for l in range(0, columns, LANES):
            lanes = slice(l, l + LANES)
            block = [ints[c, t * TILE:(t + 1) * TILE, lanes] for t in range(width // TILE)]
            if width % TILE:
                rest = ints[c, width // TILE * TILE:, lanes].astype(jnp.float32)
                rest = jnp.concatenate([rest, jnp.zeros((TILE - width % TILE, LANES), jnp.float32)], axis=0)
                block.append(rest.astype(jnp.bfloat16))
            for t, tile in enumerate(shifted(block, kept, levels, firsts[c])):
                window[c, t * TILE:(t + 1) * TILE, lanes] = tile
    for k in range(1, n_amp):
        source = lax.rem(me_a + n_amp - k, n_amp)
        pltpu.make_async_remote_copy(
            src_ref=packed, dst_ref=gathered.at[source], send_sem=g_send.at[k], recv_sem=g_recv.at[source],
            device_id={"amp": source}, device_id_type=MESH).wait_recv()

    pages = gathered[...].astype(jnp.float32)
    lhs = []
    for c in range(c_local):
        at = [(c * pieces + p) * rows for p in range(pieces)]
        cut = [pages[:, r:r + rows, :].reshape(n_amp * rows, LANES).astype(jnp.bfloat16) for r in at]
        lhs.append(jnp.concatenate(cut, axis=1)[:, :win])
    for h in range(chunks):
        total = None
        for c in range(c_local):
            block = window[c, :, h * chunk:(h + 1) * chunk]
            term = jnp.dot(lhs[c], block, preferred_element_type=jnp.float32)
            total = term if total is None else total + term
        part[h] = total.reshape(n_int, out_rows, chunk)
        for k in range(1, n_int):
            to = lax.rem(me_i + k, n_int)
            copy = pltpu.make_async_remote_copy(
                src_ref=part.at[h, to], dst_ref=landed.at[h, me_i], send_sem=r_send.at[h, k],
                recv_sem=r_recv.at[h, me_i], device_id={"int": to}, device_id_type=MESH)
            copy.start()
            sends.append(copy)
    for h in range(chunks):
        total = part[h, me_i]
        for k in range(1, n_int):
            source = lax.rem(me_i + n_int - k, n_int)
            pltpu.make_async_remote_copy(
                src_ref=part.at[h, source], dst_ref=landed.at[h, source], send_sem=r_send.at[h, k],
                recv_sem=r_recv.at[h, source], device_id={"int": source}, device_id_type=MESH).wait_recv()
            total = total + landed[h, source]
        out_ref[:, h * chunk:(h + 1) * chunk] = total
    for copy in sends:
        copy.wait_send()


def solution(mesh):
    n_amp, n_int = mesh.shape["amp"], mesh.shape["int"]

    def body(amps, integrals, irrep_sizes, c_irreps):
        rows, c_local, width = amps.shape
        columns = integrals.shape[0]
        out_rows = n_amp * rows // n_int
        chunks = chunks_of(columns)
        win = tiles_of(width)[1] * TILE
        pieces = -(-win // LANES)
        page = (c_local * pieces * rows, LANES)
        parts = (chunks, n_int, out_rows, columns // chunks)
        return pl.pallas_call(
            functools.partial(kernel, n_amp, n_int),
            out_shape=jax.ShapeDtypeStruct((out_rows, columns), jnp.float32),
            in_specs=[
                pl.BlockSpec(memory_space=pl.ANY),
            ] * 4,
            out_specs=pl.BlockSpec(memory_space=pltpu.VMEM),
            scratch_shapes=[
                pltpu.SMEM(irrep_sizes.shape, jnp.int32),
                pltpu.SMEM(c_irreps.shape, jnp.int32),
                pltpu.VMEM((c_local, rows, width), jnp.bfloat16),
                pltpu.VMEM((c_local, width, columns), jnp.bfloat16),
                pltpu.VMEM((c_local, win, columns), jnp.bfloat16),
                pltpu.VMEM(page, jnp.bfloat16),
                pltpu.VMEM((n_amp,) + page, jnp.bfloat16),
                pltpu.VMEM(parts, jnp.float32),
                pltpu.VMEM(parts, jnp.float32),
                pltpu.SemaphoreType.DMA((4,)),
                pltpu.SemaphoreType.DMA((n_amp,)),
                pltpu.SemaphoreType.DMA((n_amp,)),
                pltpu.SemaphoreType.DMA((chunks, n_int)),
                pltpu.SemaphoreType.DMA((chunks, n_int)),
            ],
            compiler_params=pltpu.CompilerParams(
                collective_id=0, has_side_effects=True, vmem_limit_bytes=63 * 1024 * 1024
            ),
            cost_estimate=pl.CostEstimate(
                flops=2 * n_amp * rows * columns * width, bytes_accessed=2 * columns * width, transcendentals=0
            ),
        )(irrep_sizes, c_irreps, jnp.transpose(amps, (1, 0, 2)), jnp.transpose(integrals, (1, 2, 0)))

    placed = (P("amp", "int", None), P("amp", "int", None), P(), P("int"))
    return jax.shard_map(
        body, mesh=mesh, in_specs=placed, out_specs=P("int", "amp"), check_vma=False
    )
```

```python
import functools

import jax
import jax.numpy as jnp
from jax import lax
from jax.experimental import pallas as pl
from jax.experimental.pallas import tpu as pltpu
from jax.sharding import PartitionSpec as P

MESH = pl.DeviceIdType.MESH
MOST = 200
TILE = 16
LANES = 128


def tiles_of(width):
    tiles = -(-width // TILE)
    return tiles, min(tiles, -(-(MOST + TILE - 1) // TILE))


def levels_of(last):
    levels = []
    while sum(levels) < last:
        levels.insert(0, 2 * levels[0] if levels else 1)
    return levels


def shifted(parts, kept, levels, first):
    for i, step in enumerate(levels):
        need = kept + sum(levels[i + 1:])
        odd = lax.rem(lax.div(first, step), 2) == 1
        parts = [
            jnp.where(odd, parts[j + step], parts[j]) if j + step < len(parts) else parts[j]
            for j in range(min(need, len(parts)))
        ]
    return parts


def chunks_of(columns):
    return 4 if columns % (4 * LANES) == 0 else 1


def kernel(n_amp, n_int, sizes_hbm, irreps, amps_hbm, ints_hbm, out_hbm, sizes, amps, ints, window, packed, gathered, part,
           local_sem, g_send, g_recv, r_send, r_recv):
    me_a, me_i = lax.axis_index("amp"), lax.axis_index("int")
    c_local, rows, width = amps.shape
    columns = ints.shape[2]
    chunks, _, out_rows, chunk = part.shape
    tiles, kept = tiles_of(width)
    levels = levels_of(tiles - kept)
    win = kept * TILE
    pieces = packed.shape[0] // (c_local * rows)

    barrier = pltpu.get_barrier_semaphore()
    for k in range(1, n_amp):
        pl.semaphore_signal(barrier, inc=1, device_id={"amp": lax.rem(me_a + k, n_amp)}, device_id_type=MESH)
    for k in range(1, n_int):
        pl.semaphore_signal(barrier, inc=1, device_id={"int": lax.rem(me_i + k, n_int)}, device_id_type=MESH)
    small = [
        pltpu.make_async_copy(sizes_hbm, sizes, local_sem.at[2]),
        pltpu.make_async_copy(amps_hbm, amps, local_sem.at[0]),
    ]
    for copy in small:
        copy.start()
    ints_in = pltpu.make_async_copy(ints_hbm, ints, local_sem.at[1])
    ints_in.start()

    firsts = []
    for copy in small:
        copy.wait()
    padded = -(-width // LANES) * LANES
    for c in range(c_local):
        irrep = irreps[c]
        start, end = jnp.int32(0), jnp.int32(0)
        for g in range(sizes.shape[0]):
            size = sizes[g]
            start += jnp.where(g < irrep, size, 0)
            end += jnp.where(g <= irrep, size, 0)
        first = jnp.minimum(lax.div(start, TILE), tiles - kept)
        firsts.append(first)
        wide = jnp.pad(amps[c].astype(jnp.float32), ((0, 0), (0, padded - width)))
        column = lax.broadcasted_iota(jnp.int32, (rows, padded), 1)
        wide = jnp.where((column >= start) & (column < end), wide, 0.0)
        for step in levels:
            odd = lax.rem(lax.div(first, step), 2) == 1
            wide = jnp.where(odd, pltpu.roll(wide, padded - step * TILE, 1), wide)
        stack = jnp.concatenate([wide[:, p * LANES:(p + 1) * LANES] for p in range(pieces)], axis=0)
        packed[c * pieces * rows:(c + 1) * pieces * rows, :] = stack.astype(jnp.bfloat16)

    pl.semaphore_wait(barrier, n_amp + n_int - 2)
    sends = []
    for k in range(1, n_amp):
        copy = pltpu.make_async_remote_copy(
            src_ref=packed, dst_ref=gathered.at[me_a], send_sem=g_send.at[k], recv_sem=g_recv.at[me_a],
            device_id={"amp": lax.rem(me_a + k, n_amp)}, device_id_type=MESH)
        copy.start()
        sends.append(copy)
    gathered[me_a] = packed[...]
    ints_in.wait()
    for c in range(c_local):
        for l in range(0, columns, LANES):
            lanes = slice(l, l + LANES)
            block = [ints[c, t * TILE:(t + 1) * TILE, lanes] for t in range(width // TILE)]
            if width % TILE:
                rest = ints[c, width // TILE * TILE:, lanes].astype(jnp.float32)
                rest = jnp.concatenate([rest, jnp.zeros((TILE - width % TILE, LANES), jnp.float32)], axis=0)
                block.append(rest.astype(jnp.bfloat16))
            for t, tile in enumerate(shifted(block, kept, levels, firsts[c])):
                window[c, t * TILE:(t + 1) * TILE, lanes] = tile
    for k in range(1, n_amp):
        source = lax.rem(me_a + n_amp - k, n_amp)
        pltpu.make_async_remote_copy(
            src_ref=packed, dst_ref=gathered.at[source], send_sem=g_send.at[k], recv_sem=g_recv.at[source],
            device_id={"amp": source}, device_id_type=MESH).wait_recv()

    pages = gathered[...].astype(jnp.float32)
    lhs = []
    for c in range(c_local):
        at = [(c * pieces + p) * rows for p in range(pieces)]
        cut = [pages[:, r:r + rows, :].reshape(n_amp * rows, LANES).astype(jnp.bfloat16) for r in at]
        lhs.append(jnp.concatenate(cut, axis=1)[:, :win])
    kept_here = []
    for h in range(chunks):
        total = None
        for c in range(c_local):
            block = window[c, :, h * chunk:(h + 1) * chunk]
            term = jnp.dot(lhs[c], block, preferred_element_type=jnp.float32)
            total = term if total is None else total + term
        part[h] = total.reshape(n_int, out_rows, chunk)
        for k in range(1, n_int):
            to = lax.rem(me_i + k, n_int)
            copy = pltpu.make_async_remote_copy(
                src_ref=part.at[h, to], dst_ref=out_hbm.at[me_i, :, h * chunk:(h + 1) * chunk], send_sem=r_send.at[h, k],
                recv_sem=r_recv.at[h, me_i], device_id={"int": to}, device_id_type=MESH)
            copy.start()
            sends.append(copy)
        copy = pltpu.make_async_copy(
            part.at[h, me_i], out_hbm.at[me_i, :, h * chunk:(h + 1) * chunk], r_recv.at[h, me_i])
        copy.start()
        kept_here.append(copy)
    for h in range(chunks):
        for k in range(1, n_int):
            source = lax.rem(me_i + n_int - k, n_int)
            pltpu.make_async_remote_copy(
                src_ref=part.at[h, source], dst_ref=out_hbm.at[source, :, h * chunk:(h + 1) * chunk],
                send_sem=r_send.at[h, k], recv_sem=r_recv.at[h, source], device_id={"int": source},
                device_id_type=MESH).wait_recv()
    for copy in kept_here:
        copy.wait()
    for copy in sends:
        copy.wait_send()


def solution(mesh):
    n_amp, n_int = mesh.shape["amp"], mesh.shape["int"]

    def body(amps, integrals, irrep_sizes, c_irreps):
        rows, c_local, width = amps.shape
        columns = integrals.shape[0]
        out_rows = n_amp * rows // n_int
        chunks = chunks_of(columns)
        win = tiles_of(width)[1] * TILE
        pieces = -(-win // LANES)
        page = (c_local * pieces * rows, LANES)
        parts = (chunks, n_int, out_rows, columns // chunks)
        addends = pl.pallas_call(
            functools.partial(kernel, n_amp, n_int),
            out_shape=jax.ShapeDtypeStruct((n_int, out_rows, columns), jnp.float32),
            in_specs=[
                pl.BlockSpec(memory_space=pl.ANY),
                pl.BlockSpec(memory_space=pltpu.SMEM),
                pl.BlockSpec(memory_space=pl.ANY),
                pl.BlockSpec(memory_space=pl.ANY),
            ],
            out_specs=pl.BlockSpec(memory_space=pl.ANY),
            scratch_shapes=[
                pltpu.SMEM(irrep_sizes.shape, jnp.int32),
                pltpu.VMEM((c_local, rows, width), jnp.bfloat16),
                pltpu.VMEM((c_local, width, columns), jnp.bfloat16),
                pltpu.VMEM((c_local, win, columns), jnp.bfloat16),
                pltpu.VMEM(page, jnp.bfloat16),
                pltpu.VMEM((n_amp,) + page, jnp.bfloat16),
                pltpu.VMEM(parts, jnp.float32),
                pltpu.SemaphoreType.DMA((3,)),
                pltpu.SemaphoreType.DMA((n_amp,)),
                pltpu.SemaphoreType.DMA((n_amp,)),
                pltpu.SemaphoreType.DMA((chunks, n_int)),
                pltpu.SemaphoreType.DMA((chunks, n_int)),
            ],
            compiler_params=pltpu.CompilerParams(
                collective_id=0, has_side_effects=True, vmem_limit_bytes=63 * 1024 * 1024
            ),
            cost_estimate=pl.CostEstimate(
                flops=2 * n_amp * rows * columns * width, bytes_accessed=2 * columns * width, transcendentals=0
            ),
        )(irrep_sizes, c_irreps, jnp.transpose(amps, (1, 0, 2)), jnp.transpose(integrals, (1, 2, 0)))
        return jnp.sum(addends, axis=0)

    placed = (P("amp", "int", None), P("amp", "int", None), P(), P("int"))
    return jax.shard_map(
        body, mesh=mesh, in_specs=placed, out_specs=P("int", "amp"), check_vma=False
    )
```

```python
import functools

import jax
import jax.numpy as jnp
from jax import lax
from jax.experimental import pallas as pl
from jax.experimental.pallas import tpu as pltpu
from jax.sharding import PartitionSpec as P

MESH = pl.DeviceIdType.MESH
MOST = 200
TILE = 16
LANES = 128


def tiles_of(width):
    tiles = -(-width // TILE)
    return tiles, min(tiles, -(-(MOST + TILE - 1) // TILE))


def levels_of(last):
    levels = []
    while sum(levels) < last:
        levels.insert(0, 2 * levels[0] if levels else 1)
    return levels


def shifted(parts, kept, levels, first):
    for i, step in enumerate(levels):
        need = kept + sum(levels[i + 1:])
        odd = lax.rem(lax.div(first, step), 2) == 1
        parts = [
            jnp.where(odd, parts[j + step], parts[j]) if j + step < len(parts) else parts[j]
            for j in range(min(need, len(parts)))
        ]
    return parts


def chunks_of(columns):
    return 2 if columns % (2 * LANES) == 0 else 1


def step_of(grade):
    return jnp.exp2(grade * (1.0 / 64.0) - 15.0)


def kernel(n_amp, n_int, sizes_hbm, irreps, amps_hbm, ints_hbm, out_ref, sizes, amps, ints, window, packed, gathered, exact, part, landed,
           local_sem, g_send, g_recv, r_send, r_recv):
    me_a, me_i = lax.axis_index("amp"), lax.axis_index("int")
    c_local, rows, width = amps.shape
    columns = ints.shape[2]
    chunks, _, out_rows, chunk = exact.shape
    tiles, kept = tiles_of(width)
    levels = levels_of(tiles - kept)
    win = kept * TILE
    pieces = packed.shape[0] // (c_local * rows)

    barrier = pltpu.get_barrier_semaphore()
    for k in range(1, n_amp):
        pl.semaphore_signal(barrier, inc=1, device_id={"amp": lax.rem(me_a + k, n_amp)}, device_id_type=MESH)
    for k in range(1, n_int):
        pl.semaphore_signal(barrier, inc=1, device_id={"int": lax.rem(me_i + k, n_int)}, device_id_type=MESH)
    small = [
        pltpu.make_async_copy(sizes_hbm, sizes, local_sem.at[2]),
        pltpu.make_async_copy(amps_hbm, amps, local_sem.at[0]),
    ]
    for copy in small:
        copy.start()
    ints_in = pltpu.make_async_copy(ints_hbm, ints, local_sem.at[1])
    ints_in.start()

    firsts = []
    for copy in small:
        copy.wait()
    padded = -(-width // LANES) * LANES
    for c in range(c_local):
        irrep = irreps[c]
        start, end = jnp.int32(0), jnp.int32(0)
        for g in range(sizes.shape[0]):
            size = sizes[g]
            start += jnp.where(g < irrep, size, 0)
            end += jnp.where(g <= irrep, size, 0)
        first = jnp.minimum(lax.div(start, TILE), tiles - kept)
        firsts.append(first)
        wide = jnp.pad(amps[c].astype(jnp.float32), ((0, 0), (0, padded - width)))
        column = lax.broadcasted_iota(jnp.int32, (rows, padded), 1)
        wide = jnp.where((column >= start) & (column < end), wide, 0.0)
        for step in levels:
            odd = lax.rem(lax.div(first, step), 2) == 1
            wide = jnp.where(odd, pltpu.roll(wide, padded - step * TILE, 1), wide)
        stack = jnp.concatenate([wide[:, p * LANES:(p + 1) * LANES] for p in range(pieces)], axis=0)
        packed[c * pieces * rows:(c + 1) * pieces * rows, :] = stack.astype(jnp.bfloat16)

    pl.semaphore_wait(barrier, n_amp + n_int - 2)
    sends = []
    for k in range(1, n_amp):
        copy = pltpu.make_async_remote_copy(
            src_ref=packed, dst_ref=gathered.at[me_a], send_sem=g_send.at[k], recv_sem=g_recv.at[me_a],
            device_id={"amp": lax.rem(me_a + k, n_amp)}, device_id_type=MESH)
        copy.start()
        sends.append(copy)
    gathered[me_a] = packed[...]
    ints_in.wait()
    for c in range(c_local):
        for l in range(0, columns, LANES):
            lanes = slice(l, l + LANES)
            block = [ints[c, t * TILE:(t + 1) * TILE, lanes] for t in range(width // TILE)]
            if width % TILE:
                rest = ints[c, width // TILE * TILE:, lanes].astype(jnp.float32)
                rest = jnp.concatenate([rest, jnp.zeros((TILE - width % TILE, LANES), jnp.float32)], axis=0)
                block.append(rest.astype(jnp.bfloat16))
            for t, tile in enumerate(shifted(block, kept, levels, firsts[c])):
                window[c, t * TILE:(t + 1) * TILE, lanes] = tile
    for k in range(1, n_amp):
        source = lax.rem(me_a + n_amp - k, n_amp)
        pltpu.make_async_remote_copy(
            src_ref=packed, dst_ref=gathered.at[source], send_sem=g_send.at[k], recv_sem=g_recv.at[source],
            device_id={"amp": source}, device_id_type=MESH).wait_recv()

    pages = gathered[...].astype(jnp.float32)
    lhs = []
    for c in range(c_local):
        at = [(c * pieces + p) * rows for p in range(pieces)]
        cut = [pages[:, r:r + rows, :].reshape(n_amp * rows, LANES).astype(jnp.bfloat16) for r in at]
        lhs.append(jnp.concatenate(cut, axis=1)[:, :win])
    for h in range(chunks):
        total = None
        for c in range(c_local):
            block = window[c, :, h * chunk:(h + 1) * chunk]
            term = jnp.dot(lhs[c], block, preferred_element_type=jnp.float32)
            total = term if total is None else total + term
        exact[h] = total.reshape(n_int, out_rows, chunk)
        top = jnp.max(jnp.abs(total), axis=1, keepdims=True)
        grade = jnp.ceil(jnp.log2(jnp.maximum(top, 2.0 ** -100)) * 64.0) + 1.0
        whole = jnp.floor(total * (1.0 / step_of(grade)) + 0.5)
        whole = jnp.minimum(jnp.maximum(whole, -32767.0), 32767.0)
        coded = jnp.concatenate([whole, jnp.broadcast_to(grade, (grade.shape[0], LANES))], axis=1)
        coded = coded.astype(jnp.int32).astype(jnp.int16)
        part[h] = coded.reshape(n_int, out_rows, chunk + LANES)
        for k in range(1, n_int):
            to = lax.rem(me_i + k, n_int)
            copy = pltpu.make_async_remote_copy(
                src_ref=part.at[h, to], dst_ref=landed.at[h, me_i], send_sem=r_send.at[h, k],
                recv_sem=r_recv.at[h, me_i], device_id={"int": to}, device_id_type=MESH)
            copy.start()
            sends.append(copy)
    for h in range(chunks):
        total = exact[h, me_i]
        for k in range(1, n_int):
            source = lax.rem(me_i + n_int - k, n_int)
            pltpu.make_async_remote_copy(
                src_ref=part.at[h, source], dst_ref=landed.at[h, source], send_sem=r_send.at[h, k],
                recv_sem=r_recv.at[h, source], device_id={"int": source}, device_id_type=MESH).wait_recv()
            coded = landed[h, source].astype(jnp.int32).astype(jnp.float32)
            step = step_of(coded[:, chunk:])
            total = total + coded[:, :chunk] * jnp.concatenate([step] * (chunk // LANES), axis=1)
        out_ref[:, h * chunk:(h + 1) * chunk] = total
    for copy in sends:
        copy.wait_send()


def solution(mesh):
    n_amp, n_int = mesh.shape["amp"], mesh.shape["int"]

    def body(amps, integrals, irrep_sizes, c_irreps):
        rows, c_local, width = amps.shape
        columns = integrals.shape[0]
        out_rows = n_amp * rows // n_int
        chunks = chunks_of(columns)
        win = tiles_of(width)[1] * TILE
        pieces = -(-win // LANES)
        page = (c_local * pieces * rows, LANES)
        parts = (chunks, n_int, out_rows, columns // chunks)
        coded = parts[:3] + (parts[3] + LANES,)
        return pl.pallas_call(
            functools.partial(kernel, n_amp, n_int),
            out_shape=jax.ShapeDtypeStruct((out_rows, columns), jnp.float32),
            in_specs=[
                pl.BlockSpec(memory_space=pl.ANY),
                pl.BlockSpec(memory_space=pltpu.SMEM),
                pl.BlockSpec(memory_space=pl.ANY),
                pl.BlockSpec(memory_space=pl.ANY),
            ],
            out_specs=pl.BlockSpec(memory_space=pltpu.VMEM),
            scratch_shapes=[
                pltpu.SMEM(irrep_sizes.shape, jnp.int32),
                pltpu.VMEM((c_local, rows, width), jnp.bfloat16),
                pltpu.VMEM((c_local, width, columns), jnp.bfloat16),
                pltpu.VMEM((c_local, win, columns), jnp.bfloat16),
                pltpu.VMEM(page, jnp.bfloat16),
                pltpu.VMEM((n_amp,) + page, jnp.bfloat16),
                pltpu.VMEM(parts, jnp.float32),
                pltpu.VMEM(coded, jnp.int16),
                pltpu.VMEM(coded, jnp.int16),
                pltpu.SemaphoreType.DMA((3,)),
                pltpu.SemaphoreType.DMA((n_amp,)),
                pltpu.SemaphoreType.DMA((n_amp,)),
                pltpu.SemaphoreType.DMA((chunks, n_int)),
                pltpu.SemaphoreType.DMA((chunks, n_int)),
            ],
            compiler_params=pltpu.CompilerParams(
                collective_id=0, has_side_effects=True, vmem_limit_bytes=63 * 1024 * 1024
            ),
            cost_estimate=pl.CostEstimate(
                flops=2 * n_amp * rows * columns * width, bytes_accessed=2 * columns * width, transcendentals=0
            ),
        )(irrep_sizes, c_irreps, jnp.transpose(amps, (1, 0, 2)), jnp.transpose(integrals, (1, 2, 0)))

    placed = (P("amp", "int", None), P("amp", "int", None), P(), P("int"))
    return jax.shard_map(
        body, mesh=mesh, in_specs=placed, out_specs=P("int", "amp"), check_vma=False
    )
```

```python
import functools

import jax
import jax.numpy as jnp
from jax import lax
from jax.experimental import pallas as pl
from jax.experimental.pallas import tpu as pltpu
from jax.sharding import PartitionSpec as P

MESH = pl.DeviceIdType.MESH
MOST = 200
TILE = 16
LANES = 128


def tiles_of(width):
    tiles = -(-width // TILE)
    return tiles, min(tiles, -(-(MOST + TILE - 1) // TILE))


def levels_of(last):
    levels = []
    while sum(levels) < last:
        levels.insert(0, 2 * levels[0] if levels else 1)
    return levels


def shifted(parts, kept, levels, first):
    for i, step in enumerate(levels):
        need = kept + sum(levels[i + 1:])
        odd = lax.rem(lax.div(first, step), 2) == 1
        parts = [
            jnp.where(odd, parts[j + step], parts[j]) if j + step < len(parts) else parts[j]
            for j in range(min(need, len(parts)))
        ]
    return parts


def chunks_of(columns):
    return 1


def step_of(grade):
    return jnp.exp2(grade * (1.0 / 64.0) - 15.0)


def kernel(n_amp, n_int, sizes_hbm, irreps, amps_hbm, ints_hbm, out_ref, sizes, amps, ints, window, packed, gathered, exact, part, landed,
           local_sem, g_send, g_recv, r_send, r_recv):
    me_a, me_i = lax.axis_index("amp"), lax.axis_index("int")
    c_local, rows, width = amps.shape
    columns = ints.shape[2]
    chunks, _, out_rows, chunk = exact.shape
    tiles, kept = tiles_of(width)
    levels = levels_of(tiles - kept)
    win = kept * TILE
    pieces = packed.shape[0] // (c_local * rows)

    barrier = pltpu.get_barrier_semaphore()
    for k in range(1, n_amp):
        pl.semaphore_signal(barrier, inc=1, device_id={"amp": lax.rem(me_a + k, n_amp)}, device_id_type=MESH)
    for k in range(1, n_int):
        pl.semaphore_signal(barrier, inc=1, device_id={"int": lax.rem(me_i + k, n_int)}, device_id_type=MESH)
    small = [
        pltpu.make_async_copy(sizes_hbm, sizes, local_sem.at[2]),
        pltpu.make_async_copy(amps_hbm, amps, local_sem.at[0]),
    ]
    for copy in small:
        copy.start()
    ints_in = pltpu.make_async_copy(ints_hbm, ints, local_sem.at[1])
    ints_in.start()

    firsts = []
    for copy in small:
        copy.wait()
    padded = -(-width // LANES) * LANES
    for c in range(c_local):
        irrep = irreps[c]
        start, end = jnp.int32(0), jnp.int32(0)
        for g in range(sizes.shape[0]):
            size = sizes[g]
            start += jnp.where(g < irrep, size, 0)
            end += jnp.where(g <= irrep, size, 0)
        first = jnp.minimum(lax.div(start, TILE), tiles - kept)
        firsts.append(first)
        wide = jnp.pad(amps[c].astype(jnp.float32), ((0, 0), (0, padded - width)))
        column = lax.broadcasted_iota(jnp.int32, (rows, padded), 1)
        wide = jnp.where((column >= start) & (column < end), wide, 0.0)
        for step in levels:
            odd = lax.rem(lax.div(first, step), 2) == 1
            wide = jnp.where(odd, pltpu.roll(wide, padded - step * TILE, 1), wide)
        stack = jnp.concatenate([wide[:, p * LANES:(p + 1) * LANES] for p in range(pieces)], axis=0)
        packed[c * pieces * rows:(c + 1) * pieces * rows, :] = stack.astype(jnp.bfloat16)

    pl.semaphore_wait(barrier, n_amp + n_int - 2)
    sends = []
    for k in range(1, n_amp):
        copy = pltpu.make_async_remote_copy(
            src_ref=packed, dst_ref=gathered.at[me_a], send_sem=g_send.at[k], recv_sem=g_recv.at[me_a],
            device_id={"amp": lax.rem(me_a + k, n_amp)}, device_id_type=MESH)
        copy.start()
        sends.append(copy)
    gathered[me_a] = packed[...]
    ints_in.wait()
    for c in range(c_local):
        for l in range(0, columns, LANES):
            lanes = slice(l, l + LANES)
            block = [ints[c, t * TILE:(t + 1) * TILE, lanes] for t in range(width // TILE)]
            if width % TILE:
                rest = ints[c, width // TILE * TILE:, lanes].astype(jnp.float32)
                rest = jnp.concatenate([rest, jnp.zeros((TILE - width % TILE, LANES), jnp.float32)], axis=0)
                block.append(rest.astype(jnp.bfloat16))
            for t, tile in enumerate(shifted(block, kept, levels, firsts[c])):
                window[c, t * TILE:(t + 1) * TILE, lanes] = tile
    for k in range(1, n_amp):
        source = lax.rem(me_a + n_amp - k, n_amp)
        pltpu.make_async_remote_copy(
            src_ref=packed, dst_ref=gathered.at[source], send_sem=g_send.at[k], recv_sem=g_recv.at[source],
            device_id={"amp": source}, device_id_type=MESH).wait_recv()

    pages = gathered[...].astype(jnp.float32)
    lhs = []
    for c in range(c_local):
        at = [(c * pieces + p) * rows for p in range(pieces)]
        cut = [pages[:, r:r + rows, :].reshape(n_amp * rows, LANES).astype(jnp.bfloat16) for r in at]
        lhs.append(jnp.concatenate(cut, axis=1)[:, :win])
    for h in range(chunks):
        total = None
        for c in range(c_local):
            block = window[c, :, h * chunk:(h + 1) * chunk]
            term = jnp.dot(lhs[c], block, preferred_element_type=jnp.float32)
            total = term if total is None else total + term
        exact[h] = total.reshape(n_int, out_rows, chunk)
        top = jnp.max(jnp.abs(total), axis=1, keepdims=True)
        grade = jnp.ceil(jnp.log2(jnp.maximum(top, 2.0 ** -100)) * 64.0) + 1.0
        whole = jnp.floor(total * (1.0 / step_of(grade)) + 0.5)
        whole = jnp.minimum(jnp.maximum(whole, -32767.0), 32767.0)
        coded = jnp.concatenate([whole, jnp.broadcast_to(grade, (grade.shape[0], LANES))], axis=1)
        coded = coded.astype(jnp.int32).astype(jnp.int16)
        part[h] = coded.reshape(n_int, out_rows, chunk + LANES)
        for k in range(1, n_int):
            to = lax.rem(me_i + k, n_int)
            copy = pltpu.make_async_remote_copy(
                src_ref=part.at[h, to], dst_ref=landed.at[h, me_i], send_sem=r_send.at[h, k],
                recv_sem=r_recv.at[h, me_i], device_id={"int": to}, device_id_type=MESH)
            copy.start()
            sends.append(copy)
    for h in range(chunks):
        total = exact[h, me_i]
        for k in range(1, n_int):
            source = lax.rem(me_i + n_int - k, n_int)
            pltpu.make_async_remote_copy(
                src_ref=part.at[h, source], dst_ref=landed.at[h, source], send_sem=r_send.at[h, k],
                recv_sem=r_recv.at[h, source], device_id={"int": source}, device_id_type=MESH).wait_recv()
            coded = landed[h, source].astype(jnp.int32).astype(jnp.float32)
            step = step_of(coded[:, chunk:])
            total = total + coded[:, :chunk] * jnp.concatenate([step] * (chunk // LANES), axis=1)
        out_ref[:, h * chunk:(h + 1) * chunk] = total
    for copy in sends:
        copy.wait_send()


def solution(mesh):
    n_amp, n_int = mesh.shape["amp"], mesh.shape["int"]

    def body(amps, integrals, irrep_sizes, c_irreps):
        rows, c_local, width = amps.shape
        columns = integrals.shape[0]
        out_rows = n_amp * rows // n_int
        chunks = chunks_of(columns)
        win = tiles_of(width)[1] * TILE
        pieces = -(-win // LANES)
        page = (c_local * pieces * rows, LANES)
        parts = (chunks, n_int, out_rows, columns // chunks)
        coded = parts[:3] + (parts[3] + LANES,)
        return pl.pallas_call(
            functools.partial(kernel, n_amp, n_int),
            out_shape=jax.ShapeDtypeStruct((out_rows, columns), jnp.float32),
            in_specs=[
                pl.BlockSpec(memory_space=pl.ANY),
                pl.BlockSpec(memory_space=pltpu.SMEM),
                pl.BlockSpec(memory_space=pl.ANY),
                pl.BlockSpec(memory_space=pl.ANY),
            ],
            out_specs=pl.BlockSpec(memory_space=pltpu.VMEM),
            scratch_shapes=[
                pltpu.SMEM(irrep_sizes.shape, jnp.int32),
                pltpu.VMEM((c_local, rows, width), jnp.bfloat16),
                pltpu.VMEM((c_local, width, columns), jnp.bfloat16),
                pltpu.VMEM((c_local, win, columns), jnp.bfloat16),
                pltpu.VMEM(page, jnp.bfloat16),
                pltpu.VMEM((n_amp,) + page, jnp.bfloat16),
                pltpu.VMEM(parts, jnp.float32),
                pltpu.VMEM(coded, jnp.int16),
                pltpu.VMEM(coded, jnp.int16),
                pltpu.SemaphoreType.DMA((3,)),
                pltpu.SemaphoreType.DMA((n_amp,)),
                pltpu.SemaphoreType.DMA((n_amp,)),
                pltpu.SemaphoreType.DMA((chunks, n_int)),
                pltpu.SemaphoreType.DMA((chunks, n_int)),
            ],
            compiler_params=pltpu.CompilerParams(
                collective_id=0, has_side_effects=True, vmem_limit_bytes=63 * 1024 * 1024
            ),
            cost_estimate=pl.CostEstimate(
                flops=2 * n_amp * rows * columns * width, bytes_accessed=2 * columns * width, transcendentals=0
            ),
        )(irrep_sizes, c_irreps, jnp.transpose(amps, (1, 0, 2)), jnp.transpose(integrals, (1, 2, 0)))

    placed = (P("amp", "int", None), P("amp", "int", None), P(), P("int"))
    return jax.shard_map(
        body, mesh=mesh, in_specs=placed, out_specs=P("int", "amp"), check_vma=False
    )
```
